128 devices in a mesh: tm: 16 (over x, z), head: 8 (over y, core).
Axes of the slice: x: 4, y: 4, z: 4, core: 2. Of those that a mesh axis runs over, the one named last changes fastest.
Arguments:
- query_in: bfloat16 [12544, 5120], P('tm', 'head'), may hold values from -6 to 6
- key_in: bfloat16 [12544, 5120], P('tm', 'head'), may hold values from -6 to 6
- value_in: bfloat16 [12544, 5120], P('tm', 'head'), may hold values from -6 to 6
- layer_grad: bfloat16 [12544, 5120], P('tm', 'head'), may hold values from -6 to 6
- out_weight: bfloat16 [5120, 5120], P('head'), may hold values from -0.078125 to 0.078125
- group_mask: int32 [16, 16], replicated, may hold values from 0 to 1, as said below
- first_group: int32 [1], replicated, may hold values from 0 to 15
Outputs:
- query_grad: bfloat16 [12544, 5120], P('tm', 'head')
- key_grad: bfloat16 [12544, 5120], P('tm', 'head')
- value_grad: bfloat16 [12544, 5120], P('tm', 'head')
The draws below stay inside these ranges and needn't reach their ends.
Inputs may be any that keep to these rules, and one draw needn't show every extreme that they name: `group_mask`: 1 on the diagonal; each entry just below the diagonal is 1 or 0; every other entry is 0.
All inputs are finite; a program needn't handle non-finite values.
Results may differ from the reference program's by a relative error of at most 0.015.
Values may be sent and summed in bfloat16 or wider, within the bound.
A program may use at most 192 MiB of HBM per device.

```python
import jax
import jax.numpy as jnp
from jax import lax

HEADS = 40
D_HEAD = 128
GROUP = 784
WIDTH = 5120
NCHUNK = 16
SEQ = 12544


def draw_query_in(key, part):
    key = jax.random.fold_in(key, 11)
    mixed = jnp.clip(1.5 * jax.random.normal(key, (SEQ, HEADS, D_HEAD), jnp.float32), -6.0, 6.0)
    return mixed.reshape(SEQ, HEADS * D_HEAD).astype(jnp.bfloat16)


def draw_key_in(key, part):
    key = jax.random.fold_in(key, 12)
    mixed = jnp.clip(1.5 * jax.random.normal(key, (SEQ, HEADS, D_HEAD), jnp.float32), -6.0, 6.0)
    return mixed.reshape(SEQ, HEADS * D_HEAD).astype(jnp.bfloat16)


def draw_group_mask(key, part):
    key = jax.random.fold_in(key, 13)
    row_ids = jnp.arange(NCHUNK, dtype=jnp.int32)[:, None]
    col_ids = jnp.arange(NCHUNK, dtype=jnp.int32)[None, :]
    kept = jax.random.randint(key, (NCHUNK, NCHUNK), 0, 2) == 1
    below = (row_ids == col_ids + 1) & kept
    return jnp.where(below | (row_ids == col_ids), 1, 0).astype(jnp.int32)


def block_scale(stream_key, shape, split, smallest, high):
    def one(position, blocks):
        heights = jax.random.uniform(jax.random.fold_in(jax.random.fold_in(stream_key, 6), position), (blocks,), jnp.float32, smallest / len(split), high / len(split))
        return jnp.repeat(jnp.exp(heights), shape[position] // blocks).reshape((-1,) + (1,) * (len(shape) - position - 1))

    gain = one(*split[0])
    for cut in split[1:]:
        gain = gain * one(*cut)
    return gain


def gaussian(own_key, extent, width, most, pieces=(), held_as=jnp.bfloat16):
    loudness = block_scale(own_key, extent, pieces, -0.22, 0.18) if pieces else 1.0
    entries = jax.random.normal(own_key, extent, jnp.float32) * width * loudness
    return jnp.minimum(jnp.maximum(entries, -most), most).astype(held_as)


def setup_inputs(seed: int = 0) -> dict:
    seeds = jax.random.split(jax.random.key(seed), 8)
    return {
        "query_in": draw_query_in(jax.random.fold_in(seeds[7], 71), 0),
        "key_in": draw_key_in(jax.random.fold_in(seeds[7], 71), 0),
        "value_in": gaussian(seeds[2], (SEQ, WIDTH), 1.0, 6.0, ((0, 16), (1, 8))),
        "layer_grad": gaussian(seeds[3], (SEQ, WIDTH), 1.0, 6.0, ((0, 16), (1, 8))),
        "out_weight": gaussian(seeds[4], (WIDTH, WIDTH), WIDTH ** -0.5, 0.078125, ((0, 8),)),
        "group_mask": draw_group_mask(jax.random.fold_in(seeds[7], 71), 0),
        "first_group": jax.random.randint(seeds[6], (1,), 0, NCHUNK).astype(jnp.int32),
    }


lowest_start = -1e30


def reference(query_in, key_in, value_in, layer_grad, out_weight, group_mask, first_group):
    scale = D_HEAD ** -0.5
    attn_grad = jnp.dot(layer_grad, out_weight.T, preferred_element_type=jnp.float32).astype(jnp.bfloat16)
    group_ids = jnp.arange(SEQ, dtype=jnp.int32) // GROUP
    group_ok = (group_mask == 1) | (jnp.arange(NCHUNK, dtype=jnp.int32)[None, :] == first_group[0])

    def by_heads(matrix):
        return matrix.reshape(SEQ, HEADS, D_HEAD).transpose(1, 0, 2)

    def one_head(inputs):
        query_h, key_h, value_h, grad_h = inputs

        def per_block(carry, block_idx):
            key_acc, value_acc = carry
            start = (block_idx * GROUP).astype(jnp.int32)
            query_b = lax.dynamic_slice_in_dim(query_h, start, GROUP, 0)
            grad_b = lax.dynamic_slice_in_dim(grad_h, start, GROUP, 0)
            allowed = group_ok[block_idx][group_ids][None, :]
            scores = scale * jnp.dot(query_b, key_h.T, preferred_element_type=jnp.float32)
            masked = jnp.where(allowed, scores, lowest_start)
            peak = jnp.max(masked, axis=1, keepdims=True)
            total = jnp.sum(jnp.where(allowed, jnp.exp(masked - peak), 0.0), axis=1, keepdims=True)
            log_sum = peak + jnp.log(total)
            probs = jnp.where(allowed, jnp.exp(jnp.where(allowed, scores - log_sum, lowest_start)), 0.0)
            dprobs = jnp.dot(grad_b, value_h.T, preferred_element_type=jnp.float32)
            delta = jnp.sum(probs * dprobs, axis=1, keepdims=True)
            probs_low = probs.astype(jnp.bfloat16)
            value_acc = value_acc + jnp.dot(probs_low.T, grad_b, preferred_element_type=jnp.float32)
            dscores = (probs * (dprobs - delta)).astype(jnp.bfloat16)
            query_part = scale * jnp.dot(dscores, key_h, preferred_element_type=jnp.float32)
            key_acc = key_acc + scale * jnp.dot(dscores.T, query_b, preferred_element_type=jnp.float32)
            return (key_acc, value_acc), query_part

        zeros = jnp.zeros((SEQ, D_HEAD), jnp.float32)
        (key_acc, value_acc), query_parts = lax.scan(per_block, (zeros, zeros), jnp.arange(NCHUNK, dtype=jnp.int32))
        return query_parts.reshape(SEQ, D_HEAD), key_acc, value_acc

    query_all, key_all, value_all = lax.map(one_head, (by_heads(query_in), by_heads(key_in), by_heads(value_in), by_heads(attn_grad)))

    def back(stacked):
        return stacked.transpose(1, 0, 2).reshape(SEQ, HEADS * D_HEAD).astype(jnp.bfloat16)

    return back(query_all), back(key_all), back(value_all)
```

```python
import functools
import math

import jax
import jax.numpy as jnp
from jax import lax
from jax.experimental import pallas as pl
from jax.experimental.pallas import tpu as pltpu
from jax.sharding import PartitionSpec as P

MESH = pl.DeviceIdType.MESH
D_HEAD = 128
SIDE = 4
CHUNK = 224
LAG = 2
SLOTS = 4
ROW_CUT = 400
VMEM_LIMIT = 60 * 1024 * 1024
LOWEST = -1e30
NT = (((1,), (1,)), ((), ()))
NN = (((1,), (0,)), ((), ()))
TN = (((0,), (0,)), ((), ()))


class Place:
    def __init__(self):
        tm, head = lax.axis_index("tm"), lax.axis_index("head")
        self.tm, self.head = tm, head
        x, z = tm // SIDE, tm % SIDE
        self.x, self.z = x, z
        self.sib_head = head + 1 - 2 * (head % 2)
        self.up_head = (head + 2) % 8
        self.down_head = (head + 6) % 8
        self.far_head = (head + 4) % 8
        self.sib = (tm, self.sib_head)
        self.up = (tm, self.up_head)
        self.down = (tm, self.down_head)
        self.after = ((tm + 1) % 16, head)
        self.before = ((tm + 15) % 16, head)
        self.zup = (x * SIDE + (z + 1) % SIDE, head)
        self.zdown = (x * SIDE + (z + 3) % SIDE, head)
        self.xup = (((x + 1) % SIDE) * SIDE + z, head)
        self.xdown = (((x + 3) % SIDE) * SIDE + z, head)


def meet(peers):
    barrier = pltpu.get_barrier_semaphore()
    for peer in peers:
        pl.semaphore_signal(barrier, inc=1, device_id=peer, device_id_type=MESH)
    pl.semaphore_wait(barrier, len(peers))


def remote(src, dst, send, recv, peer):
    return pltpu.make_async_remote_copy(
        src_ref=src, dst_ref=dst, send_sem=send, recv_sem=recv, device_id=peer, device_id_type=MESH
    )


def chunk_of(ref, c, per_head):
    rows = pl.ds(pl.multiple_of((c % per_head) * CHUNK, CHUNK), CHUNK)
    cols = pl.ds(pl.multiple_of((c // per_head) * D_HEAD, D_HEAD), D_HEAD)
    return ref.at[rows, cols]


class Chain:
    def __init__(self, slots, stage, send, recv, peer, chunks):
        self.slots, self.stage, self.send, self.recv = slots, stage, send, recv
        self.peer, self.chunks = peer, chunks
        self.steps = chunks + 2 * LAG

    def copy(self, t):
        s = lax.rem(t, SLOTS)
        return remote(
            self.stage.at[s], self.slots.at[t], self.send.at[s], self.recv.at[t], self.peer
        )

    def step(self, t, fill):
        @pl.when((t >= LAG) & (t < self.steps + LAG))
        def _():
            self.copy(t - LAG).wait_recv()

        @pl.when((t >= 0) & (t < self.steps))
        def _():
            @pl.when(t >= SLOTS)
            def _():
                self.copy(t - SLOTS).wait_send()

            fill(t, self.stage.at[lax.rem(t, SLOTS)])
            self.copy(t).start()

    def drain(self):
        def one(t, carry):
            self.copy(t).wait_send()
            return carry

        lax.fori_loop(self.steps - SLOTS, self.steps, one, 0)


def spread_fill(chain, own, per_head, at_root):
    def fill(t, stage):
        mine = chunk_of(own, jnp.minimum(t, chain.chunks - 1), per_head)

        @pl.when(t < LAG)
        def _():
            stage[...] = mine[...]

        @pl.when(t >= LAG)
        def _():
            stage[...] = lax.select(at_root, mine[...], chain.slots[t - LAG])

    return fill


def spread_result(chain, u, own, hops):
    near = lax.select(hops == 0, own, chain.slots[u])
    far = lax.select(hops == 2, chain.slots[u + LAG], chain.slots[u + 2 * LAG])
    return lax.select(hops < 2, near, far)


def gather_kernel(
    first_ref, g_hbm, w_hbm, k_hbm, v_hbm,
    do_ref, shared_ref, prev_ref,
    gathered, weight, total, kv,
    slots_x, slots_z, stage_x, stage_z,
    load_sem, side_send, side_recv, up_send, up_recv, down_send, down_recv,
    prev_send, prev_recv, x_send, x_recv, z_send, z_recv,
):
    at = Place()
    rows, width = do_ref.shape
    per_head = 2 * rows // CHUNK
    chunks = per_head * (width // D_HEAD)
    loads = [
        pltpu.make_async_copy(g_hbm, gathered.at[at.head], load_sem.at[0]),
        pltpu.make_async_copy(k_hbm, kv.at[pl.ds(0, rows)], load_sem.at[1]),
        pltpu.make_async_copy(v_hbm, kv.at[pl.ds(rows, rows)], load_sem.at[2]),
        pltpu.make_async_copy(w_hbm, weight, load_sem.at[3]),
    ]
    for load in loads:
        load.start()
    meet([at.sib, at.up, at.down, at.after, at.before, at.zup, at.zdown, at.xup, at.xdown])

    top, low = pl.ds(0, ROW_CUT), pl.ds(ROW_CUT, rows - ROW_CUT)

    def half(head, part):
        return gathered.at[head, part]

    def send(head, part, sems, n, peer):
        return remote(half(head, part), half(head, part), sems[0].at[n], sems[1].at[n], peer)

    side, up, down = (side_send, side_recv), (up_send, up_recv), (down_send, down_recv)
    loads[0].wait()
    started = []

    def go(*args):
        copy = send(*args)
        copy.start()
        started.append(copy)

    go(at.head, top, up, 0, at.up)
    go(at.head, low, down, 0, at.down)
    go(at.head, low, up, 1, at.up)
    go(at.head, top, down, 1, at.down)
    go(at.head, pl.ds(0, rows), side, 0, at.sib)
    prevs = [
        remote(k_hbm, prev_ref.at[0], prev_send.at[0], prev_recv.at[0], at.after),
        remote(v_hbm, prev_ref.at[1], prev_send.at[1], prev_recv.at[1], at.after),
    ]
    for copy in prevs:
        copy.start()
    loads[1].wait()
    loads[2].wait()

    first = first_ref[0]
    hops_x = (first // SIDE - at.x) & (SIDE - 1)
    hops_z = (first % SIDE - at.z) & (SIDE - 1)
    chain_x = Chain(slots_x, stage_x, x_send, x_recv, at.xdown, chunks)
    chain_z = Chain(slots_z, stage_z, z_send, z_recv, at.zdown, chunks)
    fill_x = spread_fill(chain_x, kv, per_head, hops_x == 0)
    fill_z = spread_fill(chain_z, shared_ref, per_head, hops_z == 0)

    def chain_step(t, carry):
        chain_x.step(t, fill_x)
        u = t - 3 * LAG

        @pl.when((u >= 0) & (u < chunks))
        def _():
            mine = chunk_of(kv, u, per_head)[...]
            chunk_of(shared_ref, u, per_head)[...] = spread_result(chain_x, u, mine, hops_x)

        chain_z.step(u, fill_z)
        w = u - 3 * LAG

        @pl.when(w >= 0)
        def _():
            mine = chunk_of(shared_ref, w, per_head)
            mine[...] = spread_result(chain_z, w, mine[...], hops_z)

        return carry

    def project(head, fresh=False):
        cols = pl.ds(pl.multiple_of(head * width, width), width)
        part = lax.dot_general(
            gathered[head], weight[:, cols], NT, preferred_element_type=jnp.float32
        )
        total[...] = part if fresh else total[...] + part

    end = chunks + 6 * LAG
    lax.fori_loop(0, 3, chain_step, 0)
    loads[3].wait()
    project(at.head, fresh=True)
    lax.fori_loop(3, 5, chain_step, 0)
    send(at.sib_head, pl.ds(0, rows), side, 0, at.sib).wait_recv()
    project(at.sib_head)
    lax.fori_loop(5, 9, chain_step, 0)
    send(at.down_head, top, up, 0, at.up).wait_recv()
    go(at.down_head, top, up, 2, at.up)
    go(at.down_head, top, side, 1, at.sib)
    send(at.up_head, low, down, 0, at.down).wait_recv()
    go(at.up_head, low, down, 2, at.down)
    go(at.up_head, low, side, 2, at.sib)
    lax.fori_loop(9, 18, chain_step, 0)
    send(at.down_head, low, up, 1, at.up).wait_recv()
    go(at.down_head, low, side, 3, at.sib)
    send(at.up_head, top, down, 1, at.down).wait_recv()
    go(at.up_head, top, side, 4, at.sib)
    project(at.down_head)
    lax.fori_loop(18, 19, chain_step, 0)
    project(at.up_head)
    lax.fori_loop(19, 21, chain_step, 0)
    down_sib, up_sib, far_sib = [h + 1 - 2 * (h % 2) for h in (at.down_head, at.up_head, at.far_head)]
    send(down_sib, top, side, 1, at.sib).wait_recv()
    send(down_sib, low, side, 3, at.sib).wait_recv()
    project(down_sib)
    lax.fori_loop(21, 22, chain_step, 0)
    send(up_sib, low, side, 2, at.sib).wait_recv()
    send(up_sib, top, side, 4, at.sib).wait_recv()
    project(up_sib)
    lax.fori_loop(22, 27, chain_step, 0)
    send(at.far_head, top, up, 2, at.up).wait_recv()
    go(at.far_head, top, side, 5, at.sib)
    send(at.far_head, low, down, 2, at.down).wait_recv()
    go(at.far_head, low, side, 6, at.sib)
    project(at.far_head)
    lax.fori_loop(27, 29, chain_step, 0)
    send(far_sib, top, side, 5, at.sib).wait_recv()
    send(far_sib, low, side, 6, at.sib).wait_recv()
    project(far_sib)
    do_ref[...] = total[...].astype(do_ref.dtype)
    lax.fori_loop(29, end, chain_step, 0)
    for copy in prevs:
        copy.wait_recv()
        copy.wait_send()
    for copy in started:
        copy.wait_send()
    chain_x.drain()
    chain_z.drain()


def gather(first_group, g, w, k, v):
    rows, width = g.shape
    chunks = (2 * rows // CHUNK) * (width // D_HEAD)
    steps = chunks + 2 * LAG
    bf = jnp.bfloat16
    dma = pltpu.SemaphoreType.DMA
    anywhere = pl.BlockSpec(memory_space=pl.ANY)
    vmem = pl.BlockSpec(memory_space=pltpu.VMEM)
    return pl.pallas_call(
        gather_kernel,
        out_shape=[
            jax.ShapeDtypeStruct((rows, width), bf),
            jax.ShapeDtypeStruct((2 * rows, width), bf),
            jax.ShapeDtypeStruct((2, rows, width), bf),
        ],
        in_specs=[pl.BlockSpec(memory_space=pltpu.SMEM)] + [anywhere] * 4,
        out_specs=[vmem, vmem, anywhere],
        scratch_shapes=[
            pltpu.VMEM((8, rows, width), bf),
            pltpu.VMEM(w.shape, bf),
            pltpu.VMEM((rows, width), jnp.float32),
            pltpu.VMEM((2 * rows, width), bf),
            pltpu.VMEM((steps, CHUNK, D_HEAD), bf),
            pltpu.VMEM((steps, CHUNK, D_HEAD), bf),
            pltpu.VMEM((SLOTS, CHUNK, D_HEAD), bf),
            pltpu.VMEM((SLOTS, CHUNK, D_HEAD), bf),
            dma((4,)),
            dma((7,)), dma((7,)), dma((3,)), dma((3,)), dma((3,)), dma((3,)),
            dma((2,)), dma((2,)),
            dma((SLOTS,)), dma((steps,)), dma((SLOTS,)), dma((steps,)),
        ],
        compiler_params=pltpu.CompilerParams(
            collective_id=0, has_side_effects=True, vmem_limit_bytes=VMEM_LIMIT
        ),
        name="gather",
    )(first_group, g, w, k, v)


def attend_kernel(
    bias_ref, q_ref, k_ref, v_ref, do_ref, shared_ref, prev_ref,
    dq_ref, own_ref, first_ref, back_ref,
    keys, values, scores, dprobs, probs_low, ds_low,
):
    rows, width = q_ref.shape
    scale = D_HEAD ** (-0.5)
    step = 112
    blocks = rows // step

    def head_body(h, carry):
        cols = pl.ds(pl.multiple_of(h * D_HEAD, D_HEAD), D_HEAD)
        keys[0:rows] = k_ref[:, cols]
        values[0:rows] = v_ref[:, cols]
        keys[rows : 2 * rows] = shared_ref[0:rows, cols]
        values[rows : 2 * rows] = shared_ref[rows : 2 * rows, cols]
        keys[2 * rows : 3 * rows] = prev_ref[0, :, cols]
        values[2 * rows : 3 * rows] = prev_ref[1, :, cols]
        q, do = q_ref[:, cols], do_ref[:, cols]

        def score_block(i, peak):
            part = pl.ds(pl.multiple_of(i * step, step), step)
            s = lax.dot_general(keys[part], q, NT, preferred_element_type=jnp.float32)
            s = s * (scale * math.log2(math.e)) + bias_ref[i // blocks]
            scores[part] = s
            return jnp.maximum(peak, jnp.max(s, axis=0, keepdims=True))

        peak = lax.fori_loop(
            0, 3 * blocks, score_block, jnp.full((1, rows), 2 * LOWEST, jnp.float32)
        )

        def weight_block(i, sums):
            part = pl.ds(pl.multiple_of(i * step, step), step)
            dp = lax.dot_general(values[part], do, NT, preferred_element_type=jnp.float32)
            e = jnp.exp2(scores[part] - peak)
            scores[part] = e
            dprobs[part] = dp
            return (
                sums[0] + jnp.sum(e, axis=0, keepdims=True),
                sums[1] + jnp.sum(e * dp, axis=0, keepdims=True),
            )

        zero = jnp.zeros((1, rows), jnp.float32)
        mass, dot = lax.fori_loop(0, 3 * blocks, weight_block, (zero, zero))
        inverse = 1.0 / mass
        delta = dot * inverse

        def grad_block(i, carry):
            part = pl.ds(pl.multiple_of(i * step, step), step)
            p = scores[part] * inverse
            probs_low[part] = p.astype(jnp.bfloat16)
            ds_low[part] = (p * (dprobs[part] - delta)).astype(jnp.bfloat16)
            return carry

        lax.fori_loop(0, 3 * blocks, grad_block, 0)
        for pair, out in enumerate((own_ref, first_ref, back_ref)):
            part = pl.ds(pair * rows, rows)
            dv = lax.dot_general(probs_low[part], do, NN, preferred_element_type=jnp.float32)
            dk = lax.dot_general(ds_low[part], q, NN, preferred_element_type=jnp.float32)
            out[0:rows, cols] = (dk * scale).astype(jnp.bfloat16)
            out[rows : 2 * rows, cols] = dv.astype(jnp.bfloat16)
        dq = lax.dot_general(ds_low[...], keys[...], TN, preferred_element_type=jnp.float32)
        dq_ref[:, cols] = (dq * scale).astype(jnp.bfloat16)
        return carry

    lax.fori_loop(0, width // D_HEAD, head_body, 0)


def attend(bias, q, k, v, do, shared, prev):
    rows, width = q.shape
    bf = jnp.bfloat16
    vmem = pl.BlockSpec(memory_space=pltpu.VMEM)
    both = jax.ShapeDtypeStruct((2 * rows, width), bf)
    return pl.pallas_call(
        attend_kernel,
        out_shape=[jax.ShapeDtypeStruct((rows, width), bf), both, both, both],
        in_specs=[pl.BlockSpec(memory_space=pltpu.SMEM)] + [vmem] * 6,
        out_specs=[vmem] * 4,
        scratch_shapes=[
            pltpu.VMEM((3 * rows, D_HEAD), bf),
            pltpu.VMEM((3 * rows, D_HEAD), bf),
            pltpu.VMEM((3 * rows, rows), jnp.float32),
            pltpu.VMEM((3 * rows, rows), jnp.float32),
            pltpu.VMEM((3 * rows, rows), bf),
            pltpu.VMEM((3 * rows, rows), bf),
        ],
        compiler_params=pltpu.CompilerParams(vmem_limit_bytes=VMEM_LIMIT),
        name="attend",
    )(bias, q, k, v, do, shared, prev)


def sum_fill(chain, own, per_head, hops):
    last = chain.chunks - 1

    def mine(t):
        return chunk_of(own, jnp.clip(t, 0, last), per_head)[...]

    def fill(t, stage):
        @pl.when(t < LAG)
        def _():
            stage[...] = mine(t)

        @pl.when(t >= LAG)
        def _():
            added = chain.slots[t - LAG] + lax.select(hops == 2, mine(t - LAG), mine(t - 2 * LAG))
            stage[...] = lax.select(hops == 3, mine(t), added)

    return fill


def return_kernel(
    first_ref, own_ref, share_ref, back_hbm,
    dk_ref, dv_ref,
    returned, part,
    slots_z, slots_x, stage_z, stage_x,
    back_send, back_recv, z_send, z_recv, x_send, x_recv,
):
    at = Place()
    rows, width = dk_ref.shape
    per_head = 2 * rows // CHUNK
    chunks = per_head * (width // D_HEAD)
    meet([at.after, at.before, at.zup, at.zdown, at.xup, at.xdown])
    back = remote(back_hbm, returned, back_send, back_recv, at.before)
    back.start()
    first = first_ref[0]
    hops_x = (first // SIDE - at.x) & (SIDE - 1)
    hops_z = (first % SIDE - at.z) & (SIDE - 1)
    mine = lax.select(first == at.tm, jnp.float32(1), jnp.float32(0))
    chain_z = Chain(slots_z, stage_z, z_send, z_recv, at.zup, chunks)
    chain_x = Chain(slots_x, stage_x, x_send, x_recv, at.xup, chunks)
    fill_z = sum_fill(chain_z, share_ref, per_head, hops_z)
    fill_x = sum_fill(chain_x, part, per_head, hops_x)

    def chain_step(t, carry):
        chain_z.step(t, fill_z)
        u = t - 3 * LAG

        @pl.when((u >= 0) & (u < chunks))
        def _():
            here = chunk_of(share_ref, u, per_head)[...]
            chunk_of(part, u, per_head)[...] = here + slots_z[u + 2 * LAG]

        chain_x.step(u, fill_x)
        w = u - 3 * LAG

        @pl.when(w >= 0)
        def _():
            here = chunk_of(part, w, per_head)
            here[...] = here[...] + slots_x[w + 2 * LAG]

        return carry

    lax.fori_loop(0, chunks + 6 * LAG, chain_step, 0)
    back.wait_recv()
    back.wait_send()
    chain_z.drain()
    chain_x.drain()
    f32 = jnp.float32
    for out, start in ((dk_ref, 0), (dv_ref, rows)):
        for r in range(0, rows, 112):
            span = pl.ds(start + r, 112)
            full = own_ref[span, :].astype(f32) + returned[span, :].astype(f32)
            full = full + lax.select(
                mine > 0.5, part[span, :].astype(f32), jnp.zeros((112, width), f32)
            )
            out[pl.ds(r, 112), :] = full.astype(out.dtype)


def give_back(first_group, own, share, back):
    rows2, width = own.shape
    rows = rows2 // 2
    chunks = (rows2 // CHUNK) * (width // D_HEAD)
    steps = chunks + 2 * LAG
    bf = jnp.bfloat16
    dma = pltpu.SemaphoreType.DMA
    vmem = pl.BlockSpec(memory_space=pltpu.VMEM)
    out = jax.ShapeDtypeStruct((rows, width), bf)
    return pl.pallas_call(
        return_kernel,
        out_shape=[out, out],
        in_specs=[pl.BlockSpec(memory_space=pltpu.SMEM), vmem, vmem, pl.BlockSpec(memory_space=pl.ANY)],
        out_specs=[vmem, vmem],
        scratch_shapes=[
            pltpu.VMEM((rows2, width), bf),
            pltpu.VMEM((rows2, width), bf),
            pltpu.VMEM((steps, CHUNK, D_HEAD), bf),
            pltpu.VMEM((steps, CHUNK, D_HEAD), bf),
            pltpu.VMEM((SLOTS, CHUNK, D_HEAD), bf),
            pltpu.VMEM((SLOTS, CHUNK, D_HEAD), bf),
            dma, dma,
            dma((SLOTS,)), dma((steps,)), dma((SLOTS,)), dma((steps,)),
        ],
        compiler_params=pltpu.CompilerParams(
            collective_id=1, has_side_effects=True, vmem_limit_bytes=VMEM_LIMIT
        ),
        name="give_back",
    )(first_group, own, share, back)


def local(query_in, key_in, value_in, layer_grad, out_weight, group_mask, first_group):
    me = lax.axis_index("tm")
    first = first_group[0]
    before = jnp.maximum(me - 1, 0)
    prev_used = (me > 0) & (group_mask[me, before] == 1) & (first != me - 1)
    used = jnp.stack([jnp.bool_(True), first != me, prev_used])
    bias = jnp.where(used, 0.0, LOWEST).astype(jnp.float32)
    do, shared, prev = gather(first_group, layer_grad, out_weight, key_in, value_in)
    dq, own, share, back = attend(bias, query_in, key_in, value_in, do, shared, prev)
    dk, dv = give_back(first_group, own, share, back)
    return dq, dk, dv


def solution(mesh):
    tiles = P("tm", "head")
    return jax.shard_map(
        local,
        mesh=mesh,
        in_specs=(tiles, tiles, tiles, tiles, P("head", None), P(), P()),
        out_specs=(tiles, tiles, tiles),
        check_vma=False,
    )
```

```python
import functools
import math

import jax
import jax.numpy as jnp
from jax import lax
from jax.experimental import pallas as pl
from jax.experimental.pallas import tpu as pltpu
from jax.sharding import PartitionSpec as P

MESH = pl.DeviceIdType.MESH
D_HEAD = 128
SIDE = 4
CHUNK = 224
LAG = 3
SLOTS = 6
ROW_CUT = 400
VMEM_LIMIT = 63 * 1024 * 1024
LOWEST = -1e30
NT = (((1,), (1,)), ((), ()))
NN = (((1,), (0,)), ((), ()))


class Place:
    def __init__(self):
        tm, head = lax.axis_index("tm"), lax.axis_index("head")
        self.tm, self.head = tm, head
        x, z = tm // SIDE, tm % SIDE
        self.x, self.z = x, z
        self.sib_head = head + 1 - 2 * (head % 2)
        self.up_head = (head + 2) % 8
        self.down_head = (head + 6) % 8
        self.far_head = (head + 4) % 8
        self.sib = (tm, self.sib_head)
        self.up = (tm, self.up_head)
        self.down = (tm, self.down_head)
        self.after = ((tm + 1) % 16, head)
        self.before = ((tm + 15) % 16, head)
        self.zup = (x * SIDE + (z + 1) % SIDE, head)
        self.zdown = (x * SIDE + (z + 3) % SIDE, head)
        self.xup = (((x + 1) % SIDE) * SIDE + z, head)
        self.xdown = (((x + 3) % SIDE) * SIDE + z, head)


def meet(peers):
    barrier = pltpu.get_barrier_semaphore()
    for peer in peers:
        pl.semaphore_signal(barrier, inc=1, device_id=peer, device_id_type=MESH)
    pl.semaphore_wait(barrier, len(peers))


def remote(src, dst, send, recv, peer):
    return pltpu.make_async_remote_copy(
        src_ref=src, dst_ref=dst, send_sem=send, recv_sem=recv, device_id=peer, device_id_type=MESH
    )


def chunk_of(ref, c, per_head):
    rows = pl.ds(pl.multiple_of((c % per_head) * CHUNK, CHUNK), CHUNK)
    cols = pl.ds(pl.multiple_of((c // per_head) * D_HEAD, D_HEAD), D_HEAD)
    return ref.at[rows, cols]


class Chain:
    def __init__(self, slots, stage, send, recv, peer, chunks):
        self.slots, self.stage, self.send, self.recv = slots, stage, send, recv
        self.peer, self.chunks = peer, chunks
        self.steps = chunks + 2 * LAG

    def copy(self, t):
        s = lax.rem(t, SLOTS)
        return remote(
            self.stage.at[s], self.slots.at[t], self.send.at[s], self.recv.at[t], self.peer
        )

    def step(self, t, fill):
        @pl.when((t >= LAG) & (t < self.steps + LAG))
        def _():
            self.copy(t - LAG).wait_recv()

        @pl.when((t >= 0) & (t < self.steps))
        def _():
            @pl.when(t >= SLOTS)
            def _():
                self.copy(t - SLOTS).wait_send()

            fill(t, self.stage.at[lax.rem(t, SLOTS)])
            self.copy(t).start()

    def drain(self):
        def one(t, carry):
            self.copy(t).wait_send()
            return carry

        lax.fori_loop(self.steps - SLOTS, self.steps, one, 0)


def spread_fill(chain, own, per_head, at_root):
    def fill(t, stage):
        mine = chunk_of(own, jnp.minimum(t, chain.chunks - 1), per_head)

        @pl.when(t < LAG)
        def _():
            stage[...] = mine[...]

        @pl.when(t >= LAG)
        def _():
            stage[...] = lax.select(at_root, mine[...], chain.slots[t - LAG])

    return fill


def spread_result(chain, u, own, hops):
    near = lax.select(hops == 0, own, chain.slots[u])
    far = lax.select(hops == 2, chain.slots[u + LAG], chain.slots[u + 2 * LAG])
    return lax.select(hops < 2, near, far)


def sum_fill(chain, own, per_head, hops):
    last = chain.chunks - 1

    def mine(t):
        return chunk_of(own, jnp.clip(t, 0, last), per_head)[...]

    def fill(t, stage):
        @pl.when(t < LAG)
        def _():
            stage[...] = mine(t)

        @pl.when(t >= LAG)
        def _():
            added = chain.slots[t - LAG] + lax.select(hops == 2, mine(t - LAG), mine(t - 2 * LAG))
            stage[...] = lax.select(hops == 3, mine(t), added)

    return fill


def fused_kernel(
    first_ref, bias_ref, q_hbm, k_hbm, v_hbm, g_hbm, w_hbm,
    dq_ref, dk_ref, dv_ref,
    gathered, weight, q_ref, kv, do_ref, shared, prev, share, back, returned,
    scores, dprobs, keys_t, dq_t,
    in_x, in_z, in_stage_x, in_stage_z, out_x, out_z, out_stage_x, out_stage_z,
    load_sem, side_send, side_recv, up_send, up_recv, down_send, down_recv,
    prev_send, prev_recv, back_send, back_recv,
    ix_send, ix_recv, iz_send, iz_recv, ox_send, ox_recv, oz_send, oz_recv,
):
    at = Place()
    f32, bf = jnp.float32, jnp.bfloat16
    rows, width = q_ref.shape
    heads = width // D_HEAD
    per_head = 2 * rows // CHUNK
    chunks = per_head * heads
    end = chunks + 6 * LAG
    loads = [
        pltpu.make_async_copy(g_hbm, gathered.at[at.head], load_sem.at[0]),
        pltpu.make_async_copy(k_hbm, kv.at[pl.ds(0, rows)], load_sem.at[1]),
        pltpu.make_async_copy(v_hbm, kv.at[pl.ds(rows, rows)], load_sem.at[2]),
        pltpu.make_async_copy(w_hbm, weight, load_sem.at[3]),
        pltpu.make_async_copy(q_hbm, q_ref, load_sem.at[4]),
    ]
    for load in loads:
        load.start()
    meet([at.sib, at.up, at.down, at.after, at.before, at.zup, at.zdown, at.xup, at.xdown])

    top, low = pl.ds(0, ROW_CUT), pl.ds(ROW_CUT, rows - ROW_CUT)
    every = pl.ds(0, rows)
    side, up, down = (side_send, side_recv), (up_send, up_recv), (down_send, down_recv)
    started = []

    def send(head, part, sems, n, peer):
        block = gathered.at[head, part]
        return remote(block, block, sems[0].at[n], sems[1].at[n], peer)

    def go(*args):
        copy = send(*args)
        copy.start()
        started.append(copy)

    def head_cols(h):
        return pl.ds(pl.multiple_of(h * D_HEAD, D_HEAD), D_HEAD)

    def prev_copy(h):
        span = (pl.ds(0, 2 * rows), head_cols(h))
        return remote(kv.at[span], prev.at[span], prev_send.at[h], prev_recv.at[h], at.after)

    def back_copy(h):
        span = (pl.ds(0, 2 * rows), head_cols(h))
        return remote(back.at[span], returned.at[span], back_send.at[h], back_recv.at[h], at.before)

    loads[0].wait()
    go(at.head, top, up, 0, at.up)
    go(at.head, low, down, 0, at.down)
    go(at.head, low, up, 1, at.up)
    go(at.head, top, down, 1, at.down)
    go(at.head, every, side, 0, at.sib)
    loads[1].wait()
    loads[2].wait()
    for h in range(heads):
        prev_copy(h).start()

    first = first_ref[0]
    hops_x = (first // SIDE - at.x) & (SIDE - 1)
    hops_z = (first % SIDE - at.z) & (SIDE - 1)
    spread_x = Chain(in_x, in_stage_x, ix_send, ix_recv, at.xdown, chunks)
    spread_z = Chain(in_z, in_stage_z, iz_send, iz_recv, at.zdown, chunks)
    sum_z = Chain(out_z, out_stage_z, oz_send, oz_recv, at.zup, chunks)
    sum_x = Chain(out_x, out_stage_x, ox_send, ox_recv, at.xup, chunks)
    spread_fill_x = spread_fill(spread_x, kv, per_head, hops_x == 0)
    spread_fill_z = spread_fill(spread_z, shared, per_head, hops_z == 0)
    sum_fill_z = sum_fill(sum_z, share, per_head, hops_z)
    sum_fill_x = sum_fill(sum_x, share, per_head, hops_x)

    def inside(u):
        return (u >= 0) & (u < chunks)

    def spread_step(t):
        spread_x.step(t, spread_fill_x)
        u = t - 3 * LAG
        w = u - 3 * LAG

        @pl.when(inside(u))
        def _():
            mine = chunk_of(kv, u, per_head)[...]
            chunk_of(shared, u, per_head)[...] = spread_result(spread_x, u, mine, hops_x)

        spread_z.step(u, spread_fill_z)

        @pl.when(inside(w))
        def _():
            mine = chunk_of(shared, w, per_head)
            mine[...] = spread_result(spread_z, w, mine[...], hops_z)

    def sum_step(t):
        sum_z.step(t, sum_fill_z)
        u = t - 3 * LAG
        w = u - 3 * LAG

        @pl.when(inside(u))
        def _():
            here = chunk_of(share, u, per_head)
            here[...] = here[...] + out_z[u + 2 * LAG]

        sum_x.step(u, sum_fill_x)

        @pl.when(inside(w))
        def _():
            here = chunk_of(share, w, per_head)
            here[...] = here[...] + out_x[w + 2 * LAG]

    def run(step, start, count):
        def one(i, carry):
            step(start + i)
            return carry

        lax.fori_loop(0, count, one, 0)

    total = scores.at[0, :, pl.ds(0, width)]

    def project(head, fresh=False):
        cols = pl.ds(pl.multiple_of(head * width, width), width)
        part = lax.dot_general(gathered[head], weight[:, cols], NT, preferred_element_type=f32)
        total[...] = part if fresh else total[...] + part

    run(spread_step, 0, 3)
    loads[3].wait()
    loads[4].wait()
    project(at.head, fresh=True)
    run(spread_step, 3, 2)
    send(at.sib_head, every, side, 0, at.sib).wait_recv()
    project(at.sib_head)
    run(spread_step, 5, 4)
    send(at.down_head, top, up, 0, at.up).wait_recv()
    go(at.down_head, top, up, 2, at.up)
    go(at.down_head, top, side, 1, at.sib)
    send(at.up_head, low, down, 0, at.down).wait_recv()
    go(at.up_head, low, down, 2, at.down)
    go(at.up_head, low, side, 2, at.sib)
    run(spread_step, 9, 9)
    send(at.down_head, low, up, 1, at.up).wait_recv()
    go(at.down_head, low, side, 3, at.sib)
    send(at.up_head, top, down, 1, at.down).wait_recv()
    go(at.up_head, top, side, 4, at.sib)
    project(at.down_head)
    run(spread_step, 18, 1)
    project(at.up_head)
    run(spread_step, 19, 2)
    down_sib, up_sib, far_sib = [
        h + 1 - 2 * (h % 2) for h in (at.down_head, at.up_head, at.far_head)
    ]
    send(down_sib, top, side, 1, at.sib).wait_recv()
    send(down_sib, low, side, 3, at.sib).wait_recv()
    project(down_sib)
    run(spread_step, 21, 1)
    send(up_sib, low, side, 2, at.sib).wait_recv()
    send(up_sib, top, side, 4, at.sib).wait_recv()
    project(up_sib)
    run(spread_step, 22, 5)
    send(at.far_head, top, up, 2, at.up).wait_recv()
    go(at.far_head, top, side, 5, at.sib)
    send(at.far_head, low, down, 2, at.down).wait_recv()
    go(at.far_head, low, side, 6, at.sib)
    project(at.far_head)
    run(spread_step, 27, 2)
    send(far_sib, top, side, 5, at.sib).wait_recv()
    send(far_sib, low, side, 6, at.sib).wait_recv()
    project(far_sib)
    do_ref[...] = total[...].astype(bf)
    for copy in started:
        copy.wait_send()
    run(spread_step, 29, 3)

    scale = D_HEAD ** (-0.5)
    unit = scale * math.log2(math.e)
    keys = (kv.at[pl.ds(0, rows)], shared.at[pl.ds(0, rows)], prev.at[pl.ds(0, rows)])
    values = (kv.at[pl.ds(rows, rows)], shared.at[pl.ds(rows, rows)], prev.at[pl.ds(rows, rows)])

    def head_body(h, carry):
        cols = head_cols(h)
        q, do = q_ref[:, cols], do_ref[:, cols]
        prev_copy(h).wait_recv()
        peak = jnp.full((1, rows), LOWEST, f32)
        for i in range(3):
            block = keys[i][:, cols]
            s = lax.dot_general(block, q, NT, preferred_element_type=f32)
            scores[i] = s
            peak = jnp.maximum(peak, jnp.max(s, axis=0, keepdims=True) + bias_ref[i])
            keys_t[:, i * rows : (i + 1) * rows] = jnp.transpose(block)
        run(spread_step, 32 + 7 * h, 2)
        run(sum_step, 7 * h - 5, 2)
        mass = jnp.zeros((1, rows), f32)
        dot = mass
        for i in range(3):
            dp = lax.dot_general(values[i][:, cols], do, NT, preferred_element_type=f32)
            e = jnp.exp2(scores[i] * unit - (peak * unit - bias_ref[i]))
            scores[i] = e
            dprobs[i] = dp
            mass += jnp.sum(e, axis=0, keepdims=True)
            dot += jnp.sum(e * dp, axis=0, keepdims=True)
        inverse = 1.0 / mass
        delta = dot * inverse
        run(spread_step, 34 + 7 * h, 2)
        run(sum_step, 7 * h - 3, 2)

        def grads(i):
            p = scores[i] * inverse
            ds = (p * (dprobs[i] - delta)).astype(bf)
            dv = lax.dot_general(p.astype(bf), do, NN, preferred_element_type=f32)
            dk = lax.dot_general(ds, q, NN, preferred_element_type=f32)
            dq = lax.dot_general(
                keys_t[:, i * rows : (i + 1) * rows], ds, NN, preferred_element_type=f32
            )
            return (dk * scale).astype(bf), dv.astype(bf), dq

        share[0:rows, cols], share[rows : 2 * rows, cols], dq_t[...] = grads(1)
        run(spread_step, 36 + 7 * h, 1)
        run(sum_step, 7 * h - 1, 2)
        back[0:rows, cols], back[rows : 2 * rows, cols], dq = grads(2)
        back_copy(h).start()
        dq_t[...] += dq
        run(spread_step, 37 + 7 * h, 1)
        run(sum_step, 7 * h + 1, 1)
        dk_ref[:, cols], dv_ref[:, cols], dq = grads(0)
        dq_ref[:, cols] = (jnp.transpose(dq_t[...] + dq) * scale).astype(bf)
        run(spread_step, 38 + 7 * h, 1)
        return carry

    lax.fori_loop(0, heads, head_body, 0)
    done = 7 * heads - 5
    run(sum_step, done, end - done)
    for h in range(heads):
        back_copy(h).wait_recv()
    mine = first == at.tm
    for out, start in ((dk_ref, 0), (dv_ref, rows)):
        for r in range(0, rows, 112):
            span, here = pl.ds(start + r, 112), pl.ds(r, 112)
            full = out[here, :].astype(f32) + returned[span, :].astype(f32)
            full = full + lax.select(mine, share[span, :].astype(f32), jnp.zeros((112, width), f32))
            out[here, :] = full.astype(bf)
    for h in range(heads):
        prev_copy(h).wait_send()
        back_copy(h).wait_send()
    for chain in (spread_x, spread_z, sum_z, sum_x):
        chain.drain()


def fused(first_group, bias, q, k, v, g, w):
    rows, width = q.shape
    heads = width // D_HEAD
    chunks = (2 * rows // CHUNK) * heads
    steps = chunks + 2 * LAG
    bf = jnp.bfloat16
    dma = pltpu.SemaphoreType.DMA
    smem = pl.BlockSpec(memory_space=pltpu.SMEM)
    anywhere = pl.BlockSpec(memory_space=pl.ANY)
    vmem = pl.BlockSpec(memory_space=pltpu.VMEM)
    out = jax.ShapeDtypeStruct((rows, width), bf)
    both = pltpu.VMEM((2 * rows, width), bf)
    slots = pltpu.VMEM((steps, CHUNK, D_HEAD), bf)
    stage = pltpu.VMEM((SLOTS, CHUNK, D_HEAD), bf)
    return pl.pallas_call(
        fused_kernel,
        out_shape=[out] * 3,
        in_specs=[smem] * 2 + [anywhere] * 5,
        out_specs=[vmem] * 3,
        scratch_shapes=[
            pltpu.VMEM((8, rows, width), bf),
            pltpu.VMEM(w.shape, bf),
            pltpu.VMEM((rows, width), bf),
            both,
            pltpu.VMEM((rows, width), bf),
            both, both, both, both, both,
            pltpu.VMEM((3, rows, rows), jnp.float32),
            pltpu.VMEM((3, rows, rows), jnp.float32),
            pltpu.VMEM((D_HEAD, 3 * rows), bf),
            pltpu.VMEM((D_HEAD, rows), jnp.float32),
            slots, slots, stage, stage, slots, slots, stage, stage,
            dma((5,)),
            dma((7,)), dma((7,)), dma((3,)), dma((3,)), dma((3,)), dma((3,)),
            dma((heads,)), dma((heads,)), dma((heads,)), dma((heads,)),
        ]
        + [dma((SLOTS,)), dma((steps,))] * 4,
        compiler_params=pltpu.CompilerParams(
            collective_id=0, has_side_effects=True, vmem_limit_bytes=VMEM_LIMIT
        ),
        name="fused",
    )(first_group, bias, q, k, v, g, w)


def local(query_in, key_in, value_in, layer_grad, out_weight, group_mask, first_group):
    me = lax.axis_index("tm")
    first = first_group[0]
    before = jnp.maximum(me - 1, 0)
    prev_used = (me > 0) & (group_mask[me, before] == 1) & (first != me - 1)
    used = jnp.stack([jnp.bool_(True), first != me, prev_used])
    bias = jnp.where(used, 0.0, LOWEST).astype(jnp.float32)
    dq, dk, dv = fused(first_group, bias, query_in, key_in, value_in, layer_grad, out_weight)
    return dq, dk, dv


def solution(mesh):
    tiles = P("tm", "head")
    return jax.shard_map(
        local,
        mesh=mesh,
        in_specs=(tiles, tiles, tiles, tiles, P("head", None), P(), P()),
        out_specs=(tiles, tiles, tiles),
        check_vma=False,
    )
```

```python
import functools
import math

import jax
import jax.numpy as jnp
from jax import lax
from jax.experimental import pallas as pl
from jax.experimental.pallas import tpu as pltpu
from jax.sharding import PartitionSpec as P

MESH = pl.DeviceIdType.MESH
D_HEAD = 128
SIDE = 4
CHUNK = 224
LAG = 3
SLOTS = 6
ROW_CUT = 400
VMEM_LIMIT = 63 * 1024 * 1024
LOWEST = -1e30
BACK_LAG = 12
FINISH_ROWS = 784
NT = (((1,), (1,)), ((), ()))
NN = (((1,), (0,)), ((), ()))


class Place:
    def __init__(self):
        tm, head = lax.axis_index("tm"), lax.axis_index("head")
        self.tm, self.head = tm, head
        x, z = tm // SIDE, tm % SIDE
        self.x, self.z = x, z
        self.sib_head = head + 1 - 2 * (head % 2)
        self.up_head = (head + 2) % 8
        self.down_head = (head + 6) % 8
        self.far_head = (head + 4) % 8
        self.sib = (tm, self.sib_head)
        self.up = (tm, self.up_head)
        self.down = (tm, self.down_head)
        self.after = ((tm + 1) % 16, head)
        self.before = ((tm + 15) % 16, head)
        self.zup = (x * SIDE + (z + 1) % SIDE, head)
        self.zdown = (x * SIDE + (z + 3) % SIDE, head)
        self.xup = (((x + 1) % SIDE) * SIDE + z, head)
        self.xdown = (((x + 3) % SIDE) * SIDE + z, head)


def meet(peers):
    barrier = pltpu.get_barrier_semaphore()
    for peer in peers:
        pl.semaphore_signal(barrier, inc=1, device_id=peer, device_id_type=MESH)
    pl.semaphore_wait(barrier, len(peers))


def remote(src, dst, send, recv, peer):
    return pltpu.make_async_remote_copy(
        src_ref=src, dst_ref=dst, send_sem=send, recv_sem=recv, device_id=peer, device_id_type=MESH
    )


def chunk_of(ref, c, per_head):
    rows = pl.ds(pl.multiple_of((c % per_head) * CHUNK, CHUNK), CHUNK)
    cols = pl.ds(pl.multiple_of((c // per_head) * D_HEAD, D_HEAD), D_HEAD)
    return ref.at[rows, cols]


class Chain:
    def __init__(self, slots, stage, send, recv, peer, chunks):
        self.slots, self.stage, self.send, self.recv = slots, stage, send, recv
        self.peer, self.chunks = peer, chunks
        self.steps = chunks + 2 * LAG

    def copy(self, t):
        s = lax.rem(t, SLOTS)
        return remote(
            self.stage.at[s], self.slots.at[t], self.send.at[s], self.recv.at[t], self.peer
        )

    def step(self, t, fill):
        @pl.when((t >= LAG) & (t < self.steps + LAG))
        def _():
            self.copy(t - LAG).wait_recv()

        @pl.when((t >= 0) & (t < self.steps))
        def _():
            @pl.when(t >= SLOTS)
            def _():
                self.copy(t - SLOTS).wait_send()

            fill(t, self.stage.at[lax.rem(t, SLOTS)])
            self.copy(t).start()

    def drain(self):
        def one(t, carry):
            self.copy(t).wait_send()
            return carry

        lax.fori_loop(self.steps - SLOTS, self.steps, one, 0)


def spread_fill(chain, own, per_head, at_root):
    def fill(t, stage):
        mine = chunk_of(own, jnp.minimum(t, chain.chunks - 1), per_head)

        @pl.when(t < LAG)
        def _():
            stage[...] = mine[...]

        @pl.when(t >= LAG)
        def _():
            stage[...] = lax.select(at_root, mine[...], chain.slots[t - LAG])

    return fill


def spread_result(chain, u, own, hops):
    near = lax.select(hops == 0, own, chain.slots[u])
    far = lax.select(hops == 2, chain.slots[u + LAG], chain.slots[u + 2 * LAG])
    return lax.select(hops < 2, near, far)


def sum_fill(chain, own, per_head, hops):
    last = chain.chunks - 1

    def mine(t):
        return chunk_of(own, jnp.clip(t, 0, last), per_head)[...]

    def fill(t, stage):
        @pl.when(t < LAG)
        def _():
            stage[...] = mine(t)

        @pl.when(t >= LAG)
        def _():
            added = chain.slots[t - LAG] + lax.select(hops == 2, mine(t - LAG), mine(t - 2 * LAG))
            stage[...] = lax.select(hops == 3, mine(t), added)

    return fill


def fused_kernel(
    first_ref, mask_ref, q_hbm, k_hbm, v_hbm, g_hbm, w_hbm,
    dq_ref, own_ref, share, returned,
    gathered, weight, q_ref, kv, do_ref, shared, prev, back,
    scores, dprobs, keys_t, dq_t,
    in_x, in_z, in_stage_x, in_stage_z, out_x, out_z, out_stage_x, out_stage_z,
    load_sem, side_send, side_recv, up_send, up_recv, down_send, down_recv,
    prev_send, prev_recv, back_send, back_recv,
    ix_send, ix_recv, iz_send, iz_recv, ox_send, ox_recv, oz_send, oz_recv,
):
    at = Place()
    f32, bf = jnp.float32, jnp.bfloat16
    rows, width = q_ref.shape
    heads = width // D_HEAD
    per_head = 2 * rows // CHUNK
    chunks = per_head * heads
    end = chunks + 6 * LAG
    loads = [
        pltpu.make_async_copy(g_hbm, gathered.at[at.head], load_sem.at[0]),
        pltpu.make_async_copy(k_hbm, kv.at[pl.ds(0, rows)], load_sem.at[1]),
        pltpu.make_async_copy(v_hbm, kv.at[pl.ds(rows, rows)], load_sem.at[2]),
        pltpu.make_async_copy(w_hbm, weight, load_sem.at[3]),
        pltpu.make_async_copy(q_hbm, q_ref, load_sem.at[4]),
    ]
    for load in loads:
        load.start()
    meet([at.sib, at.up, at.down, at.after, at.before, at.zup, at.zdown, at.xup, at.xdown])

    top, low = pl.ds(0, ROW_CUT), pl.ds(ROW_CUT, rows - ROW_CUT)
    every = pl.ds(0, rows)
    side, up, down = (side_send, side_recv), (up_send, up_recv), (down_send, down_recv)
    started = []

    def send(head, part, sems, n, peer):
        block = gathered.at[head, part]
        return remote(block, block, sems[0].at[n], sems[1].at[n], peer)

    def go(*args):
        copy = send(*args)
        copy.start()
        started.append(copy)

    def head_cols(h):
        return pl.ds(pl.multiple_of(h * D_HEAD, D_HEAD), D_HEAD)

    def prev_copy(h):
        span = (pl.ds(0, 2 * rows), head_cols(h))
        return remote(kv.at[span], prev.at[span], prev_send.at[h], prev_recv.at[h], at.after)

    def back_copy(c):
        src, dst = chunk_of(back, c, per_head), chunk_of(returned, c, per_head)
        return remote(src, dst, back_send, back_recv, at.before)

    back_all = remote(back, returned, back_send, back_recv, at.before)

    loads[0].wait()
    go(at.head, top, up, 0, at.up)
    go(at.head, low, down, 0, at.down)
    go(at.head, low, up, 1, at.up)
    go(at.head, top, down, 1, at.down)
    go(at.head, every, side, 0, at.sib)
    loads[1].wait()
    loads[2].wait()
    for h in range(heads):
        prev_copy(h).start()

    first = first_ref[0]
    used = (mask_ref[at.tm, jnp.maximum(at.tm - 1, 0)] == 1) & (at.tm > 0) & (first != at.tm - 1)
    bias = (
        jnp.float32(0),
        lax.select(first != at.tm, jnp.float32(0), jnp.float32(LOWEST)),
        lax.select(used, jnp.float32(0), jnp.float32(LOWEST)),
    )
    hops_x = (first // SIDE - at.x) & (SIDE - 1)
    hops_z = (first % SIDE - at.z) & (SIDE - 1)
    spread_x = Chain(in_x, in_stage_x, ix_send, ix_recv, at.xdown, chunks)
    spread_z = Chain(in_z, in_stage_z, iz_send, iz_recv, at.zdown, chunks)
    sum_z = Chain(out_z, out_stage_z, oz_send, oz_recv, at.zup, chunks)
    sum_x = Chain(out_x, out_stage_x, ox_send, ox_recv, at.xup, chunks)
    spread_fill_x = spread_fill(spread_x, kv, per_head, hops_x == 0)
    spread_fill_z = spread_fill(spread_z, shared, per_head, hops_z == 0)
    sum_fill_z = sum_fill(sum_z, share, per_head, hops_z)
    sum_fill_x = sum_fill(sum_x, share, per_head, hops_x)

    def inside(u):
        return (u >= 0) & (u < chunks)

    def spread_step(t):
        spread_x.step(t, spread_fill_x)
        u = t - 3 * LAG
        w = u - 3 * LAG

        @pl.when(inside(u))
        def _():
            mine = chunk_of(kv, u, per_head)[...]
            chunk_of(shared, u, per_head)[...] = spread_result(spread_x, u, mine, hops_x)

        spread_z.step(u, spread_fill_z)

        @pl.when(inside(w))
        def _():
            mine = chunk_of(shared, w, per_head)
            mine[...] = spread_result(spread_z, w, mine[...], hops_z)

    def sum_step(t):
        sum_z.step(t, sum_fill_z)
        pl.when(inside(t - BACK_LAG))(lambda: back_copy(t - BACK_LAG).start())
        u = t - 3 * LAG
        w = u - 3 * LAG

        @pl.when(inside(u))
        def _():
            here = chunk_of(share, u, per_head)
            here[...] = here[...] + out_z[u + 2 * LAG]

        sum_x.step(u, sum_fill_x)

        @pl.when(inside(w))
        def _():
            here = chunk_of(share, w, per_head)
            here[...] = here[...] + out_x[w + 2 * LAG]

    def run(step, start, count):
        def one(i, carry):
            step(start + i)
            return carry

        lax.fori_loop(0, count, one, 0)

    total = scores.at[0, :, pl.ds(0, width)]

    def project(head, fresh=False):
        cols = pl.ds(pl.multiple_of(head * width, width), width)
        part = lax.dot_general(gathered[head], weight[:, cols], NT, preferred_element_type=f32)
        total[...] = part if fresh else total[...] + part

    run(spread_step, 0, 3)
    loads[3].wait()
    loads[4].wait()
    project(at.head, fresh=True)
    run(spread_step, 3, 2)
    send(at.sib_head, every, side, 0, at.sib).wait_recv()
    project(at.sib_head)
    run(spread_step, 5, 4)
    send(at.down_head, top, up, 0, at.up).wait_recv()
    go(at.down_head, top, up, 2, at.up)
    go(at.down_head, top, side, 1, at.sib)
    send(at.up_head, low, down, 0, at.down).wait_recv()
    go(at.up_head, low, down, 2, at.down)
    go(at.up_head, low, side, 2, at.sib)
    run(spread_step, 9, 9)
    send(at.down_head, low, up, 1, at.up).wait_recv()
    go(at.down_head, low, side, 3, at.sib)
    send(at.up_head, top, down, 1, at.down).wait_recv()
    go(at.up_head, top, side, 4, at.sib)
    project(at.down_head)
    run(spread_step, 18, 1)
    project(at.up_head)
    run(spread_step, 19, 2)
    down_sib, up_sib, far_sib = [
        h + 1 - 2 * (h % 2) for h in (at.down_head, at.up_head, at.far_head)
    ]
    send(down_sib, top, side, 1, at.sib).wait_recv()
    send(down_sib, low, side, 3, at.sib).wait_recv()
    project(down_sib)
    run(spread_step, 21, 1)
    send(up_sib, low, side, 2, at.sib).wait_recv()
    send(up_sib, top, side, 4, at.sib).wait_recv()
    project(up_sib)
    run(spread_step, 22, 5)
    send(at.far_head, top, up, 2, at.up).wait_recv()
    go(at.far_head, top, side, 5, at.sib)
    send(at.far_head, low, down, 2, at.down).wait_recv()
    go(at.far_head, low, side, 6, at.sib)
    project(at.far_head)
    run(spread_step, 27, 2)
    send(far_sib, top, side, 5, at.sib).wait_recv()
    send(far_sib, low, side, 6, at.sib).wait_recv()
    project(far_sib)
    do_ref[...] = total[...].astype(bf)
    for copy in started:
        copy.wait_send()
    run(spread_step, 29, 3)

    scale = D_HEAD ** (-0.5)
    unit = scale * math.log2(math.e)
    keys = (kv.at[pl.ds(0, rows)], shared.at[pl.ds(0, rows)], prev.at[pl.ds(0, rows)])
    values = (kv.at[pl.ds(rows, rows)], shared.at[pl.ds(rows, rows)], prev.at[pl.ds(rows, rows)])

    def head_body(h, carry):
        cols = head_cols(h)
        q, do = q_ref[:, cols], do_ref[:, cols]
        prev_copy(h).wait_recv()
        peak = jnp.full((1, rows), LOWEST, f32)
        for i in range(3):
            block = keys[i][:, cols]
            s = lax.dot_general(block, q, NT, preferred_element_type=f32)
            scores[i] = s
            peak = jnp.maximum(peak, jnp.max(s, axis=0, keepdims=True) + bias[i])
            keys_t[:, i * rows : (i + 1) * rows] = jnp.transpose(block)
        run(spread_step, 32 + 7 * h, 2)
        run(sum_step, 7 * h - 5, 2)
        mass = jnp.zeros((1, rows), f32)
        dot = mass
        for i in range(3):
            dp = lax.dot_general(values[i][:, cols], do, NT, preferred_element_type=f32)
            e = jnp.exp2(scores[i] * unit - (peak * unit - bias[i]))
            scores[i] = e
            dprobs[i] = dp
            mass += jnp.sum(e, axis=0, keepdims=True)
            dot += jnp.sum(e * dp, axis=0, keepdims=True)
        inverse = 1.0 / mass
        delta = dot * inverse
        run(spread_step, 34 + 7 * h, 2)
        run(sum_step, 7 * h - 3, 2)

        def grads(i):
            p = scores[i] * inverse
            ds = (p * (dprobs[i] - delta)).astype(bf)
            dv = lax.dot_general(p.astype(bf), do, NN, preferred_element_type=f32)
            dk = lax.dot_general(ds, q, NN, preferred_element_type=f32)
            dq = lax.dot_general(
                keys_t[:, i * rows : (i + 1) * rows], ds, NN, preferred_element_type=f32
            )
            return (dk * scale).astype(bf), dv.astype(bf), dq

        share[0:rows, cols], share[rows : 2 * rows, cols], dq_t[...] = grads(1)
        run(spread_step, 36 + 7 * h, 1)
        run(sum_step, 7 * h - 1, 2)
        back[0:rows, cols], back[rows : 2 * rows, cols], dq = grads(2)
        dq_t[...] += dq
        run(spread_step, 37 + 7 * h, 1)
        run(sum_step, 7 * h + 1, 1)
        own_ref[0:rows, cols], own_ref[rows : 2 * rows, cols], dq = grads(0)
        dq_ref[:, cols] = (jnp.transpose(dq_t[...] + dq) * scale).astype(bf)
        run(spread_step, 38 + 7 * h, 1)
        return carry

    lax.fori_loop(0, heads, head_body, 0)
    done = 7 * heads - 5
    run(sum_step, done, end - done)
    back_all.wait_recv()
    for h in range(heads):
        prev_copy(h).wait_send()
    back_all.wait_send()
    for chain in (spread_x, spread_z, sum_z, sum_x):
        chain.drain()


def fused(first_group, group_mask, q, k, v, g, w):
    rows, width = q.shape
    heads = width // D_HEAD
    chunks = (2 * rows // CHUNK) * heads
    steps = chunks + 2 * LAG
    bf = jnp.bfloat16
    dma = pltpu.SemaphoreType.DMA
    smem = pl.BlockSpec(memory_space=pltpu.SMEM)
    anywhere = pl.BlockSpec(memory_space=pl.ANY)
    vmem = pl.BlockSpec(memory_space=pltpu.VMEM)
    out = jax.ShapeDtypeStruct((rows, width), bf)
    out2 = jax.ShapeDtypeStruct((2 * rows, width), bf)
    both = pltpu.VMEM((2 * rows, width), bf)
    slots = pltpu.VMEM((steps, CHUNK, D_HEAD), bf)
    stage = pltpu.VMEM((SLOTS, CHUNK, D_HEAD), bf)
    return pl.pallas_call(
        fused_kernel,
        out_shape=[out, out2, out2, out2],
        in_specs=[smem] * 2 + [anywhere] * 5,
        out_specs=[vmem] * 3 + [anywhere],
        scratch_shapes=[
            pltpu.VMEM((8, rows, width), bf),
            pltpu.VMEM(w.shape, bf),
            pltpu.VMEM((rows, width), bf),
            both,
            pltpu.VMEM((rows, width), bf),
            both, both, both,
            pltpu.VMEM((3, rows, rows), jnp.float32),
            pltpu.VMEM((3, rows, rows), jnp.float32),
            pltpu.VMEM((D_HEAD, 3 * rows), bf),
            pltpu.VMEM((D_HEAD, rows), jnp.float32),
            slots, slots, stage, stage, slots, slots, stage, stage,
            dma((5,)),
            dma((7,)), dma((7,)), dma((3,)), dma((3,)), dma((3,)), dma((3,)),
            dma((heads,)), dma((heads,)), dma, dma,
        ]
        + [dma((SLOTS,)), dma((steps,))] * 4,
        compiler_params=pltpu.CompilerParams(
            collective_id=0, has_side_effects=True, vmem_limit_bytes=VMEM_LIMIT
        ),
        name="fused",
    )(first_group, group_mask, q, k, v, g, w)


def finish_kernel(
    first_ref, dq_in, own_k, own_v, back_k, back_v, sum_k, sum_v, dq_ref, dk_ref, dv_ref
):
    f32 = jnp.float32
    mine = first_ref[0] == lax.axis_index("tm")
    dq_ref[...] = dq_in[...]
    for out, own, back, total in ((dk_ref, own_k, back_k, sum_k), (dv_ref, own_v, back_v, sum_v)):
        full = own[...].astype(f32) + back[...].astype(f32)
        full = full + lax.select(mine, total[...].astype(f32), jnp.zeros(out.shape, f32))
        out[...] = full.astype(out.dtype)


def finish(first_group, dq, own, share, returned):
    rows, width = dq.shape
    step = FINISH_ROWS
    blocks = rows // step
    upper = pl.BlockSpec((step, width), lambda i: (i, 0))
    lower = pl.BlockSpec((step, width), lambda i: (i + blocks, 0))
    out = jax.ShapeDtypeStruct((rows, width), dq.dtype)
    return pl.pallas_call(
        finish_kernel,
        grid=(blocks,),
        out_shape=[out] * 3,
        in_specs=[pl.BlockSpec(memory_space=pltpu.SMEM), upper] + [upper, lower] * 3,
        out_specs=[upper] * 3,
        compiler_params=pltpu.CompilerParams(vmem_limit_bytes=VMEM_LIMIT),
        name="finish",
    )(first_group, dq, own, own, returned, returned, share, share)


def local(query_in, key_in, value_in, layer_grad, out_weight, group_mask, first_group):
    dq, own, share, returned = fused(
        first_group, group_mask, query_in, key_in, value_in, layer_grad, out_weight
    )
    return tuple(finish(first_group, dq, own, share, returned))


def solution(mesh):
    tiles = P("tm", "head")
    return jax.shard_map(
        local,
        mesh=mesh,
        in_specs=(tiles, tiles, tiles, tiles, P("head", None), P(), P()),
        out_specs=(tiles, tiles, tiles),
        check_vma=False,
    )
```
